512 devices in a mesh: img: 32 (over z, core), orb: 16 (over y, x).
Axes of the slice: x: 4, y: 4, z: 16, core: 2. Of those that a mesh axis runs over, the one named last changes fastest.
Arguments:
- green_k: float32 [64, 8, 2, 256, 256], P('img', None, None, 'orb'), may hold values from -48 to 48
- band_of_image: int32 [64], P('img'), may hold values from 0 to 31
- fit_tensor: bfloat16 [32, 2048, 256], P(None, 'orb'), may hold values from -0.125 to 0.125
Outputs:
- sigma: float32 [64, 8, 256, 256], P('img', None, 'orb')
The draws below stay inside these ranges and needn't reach their ends.
All inputs are finite; a program needn't handle non-finite values.
Results may differ from the reference program's by a relative error of at most 0.0041.
Values may be sent and summed in bfloat16 or wider, within the bound.
No kernel may reach another device: no remote copies, remote signals or barrier semaphores. Data moves between devices by JAX's collectives and lax.ppermute only.
A program may use at most 64 MiB of HBM per device.

```python
import math
import jax
import jax.numpy as jnp
from jax import lax

NORB = 256
NAUX = 2048
TAU = 8
NBAND = 32
K_DEV = 2
NK = 64


def set_ends(result, stream_key, low, top_value):
    shape = result.shape
    index_at = [jax.random.randint(jax.random.fold_in(stream_key, axis), (), 0, shape[axis]) for axis in range(len(shape))]
    result = result.at[tuple(index_at)].set(low)
    longest = shape.index(max(shape))
    index_at[longest] = (index_at[longest] + 1) % shape[longest]
    return result.at[tuple(index_at)].set(top_value)


def steps_of(own_key, dims, split, smallest, largest):
    loudness = 1.0
    for dim, shards_of in split:
        steps = jax.random.uniform(jax.random.fold_in(jax.random.fold_in(own_key, 6), dim), (shards_of,), jnp.float32, smallest / len(split), largest / len(split))
        loudness = loudness * jnp.repeat(jnp.exp(steps), dims[dim] // shards_of).reshape((-1,) + (1,) * (len(dims) - 1 - dim))
    return loudness


def scatter_about(own_key, extent, deviation, bound, pieces=(), kind=jnp.bfloat16):
    values = deviation * jax.random.normal(own_key, extent, jnp.float32)
    if pieces:
        values = values * steps_of(own_key, extent, pieces, -0.22, 0.18)
    return jnp.clip(values, -bound, bound).astype(kind)


def setup_inputs(seed: int = 0) -> dict:
    key_list = jax.random.split(jax.random.key(seed), 4)
    green_k = scatter_about(key_list[0], (NK, TAU, 2, NORB, NORB), (NK ** 0.5), 48.0, ((0, 32), (3, 16)), jnp.float32)
    band_of_image = set_ends(jax.random.randint(key_list[1], (NK,), 0, NBAND), jax.random.fold_in(key_list[1], 1), 0, NBAND - 1).astype(jnp.int32)
    fit_tensor = scatter_about(key_list[2], (NBAND, NAUX, NORB), NAUX ** -0.5, 0.125, ((1, 16),))
    return dict(green_k=green_k, band_of_image=band_of_image, fit_tensor=fit_tensor)


def mesh_phase(count, depth):
    wide = min(8, count // depth)
    tall = count // (depth * wide)
    steps = jnp.arange(count, dtype=jnp.int32)
    first = steps // (tall * depth)
    second = (steps // depth) % tall
    third = steps % depth
    frac = ((first[:, None] * first[None, :]) % wide).astype(jnp.float32) / float(wide)
    frac = frac + ((second[:, None] * second[None, :]) % tall).astype(jnp.float32) / float(tall)
    frac = frac + ((third[:, None] * third[None, :]) % depth).astype(jnp.float32) / float(depth)
    return frac * (2.0 * math.pi)


def reference(green_k, band_of_image, fit_tensor):
    count = green_k.shape[0]
    norb = green_k.shape[3]
    phase = mesh_phase(count, K_DEV)
    cosine = jnp.cos(phase)
    sine = jnp.sin(phase)

    def transform(block):
        real_part = block[:, 0].reshape(count, -1)
        imag_part = block[:, 1].reshape(count, -1)
        summed = jnp.dot(cosine, real_part, precision=lax.Precision.HIGHEST) - jnp.dot(sine, imag_part, precision=lax.Precision.HIGHEST)
        return (summed / count).reshape(count, norb, norb)

    images = lax.map(transform, jnp.moveaxis(green_k, 1, 0))

    def integral(factor):
        return lax.dot_general(factor, factor, (((0,), (0,)), ((), ())), preferred_element_type=jnp.float32).astype(jnp.bfloat16)

    band_integral = lax.map(integral, fit_tensor)

    def one_image(index):
        weights = band_integral[band_of_image[index]].astype(jnp.float32)
        green = images[:, index]
        green_low = green.astype(jnp.bfloat16).astype(jnp.float32)
        left = jnp.einsum('tij,jk->tik', green_low, weights)
        return left * green[::-1]

    return lax.map(one_image, jnp.arange(count, dtype=jnp.int32))
```

```python
import functools

import jax
import jax.numpy as jnp
from jax import lax
from jax.experimental import pallas as pl
from jax.experimental.pallas import tpu as pltpu
from jax.sharding import PartitionSpec as P

TAU = 8
LANES = 128
HALF = 8
SIDE = 4
VMEM = pl.BlockSpec(memory_space=pltpu.VMEM)
LIMIT = 16 * 1024 * 1024


def params(limit=LIMIT):
    return pltpu.CompilerParams(vmem_limit_bytes=limit)


def cost(flops, moved):
    return pl.CostEstimate(flops=flops, bytes_accessed=moved, transcendentals=0)


def pack_kernel(band_ref, green_ref, fit_ref, packed_ref, factor_ref):
    for t in range(TAU):
        for ih in range(2):
            rows = slice(ih * HALF, (ih + 1) * HALF)
            for jh in range(2):
                cols = slice(jh * LANES, (jh + 1) * LANES)
                both = green_ref[0, t, :, rows, cols].reshape(2 * HALF, LANES)
                packed_ref[(t * 2 + ih) * 2 + jh] = both.astype(jnp.bfloat16)
    factor_ref[...] = fit_ref[...]


def pack(green_k, band, fit):
    points = green_k.shape[0]
    return pl.pallas_call(
        pack_kernel,
        grid_spec=pltpu.PrefetchScalarGridSpec(
            num_scalar_prefetch=1,
            grid=(points,),
            in_specs=[
                pl.BlockSpec((1,) + green_k.shape[1:], lambda p, band: (p, 0, 0, 0, 0)),
                pl.BlockSpec((1,) + fit.shape[1:], lambda p, band: (band[p], 0, 0)),
            ],
            out_specs=[
                pl.BlockSpec((32, 2 * HALF, LANES), lambda p, band: (0, p, 0)),
                pl.BlockSpec((1,) + fit.shape[1:], lambda p, band: (p, 0, 0)),
            ],
        ),
        out_shape=[
            jax.ShapeDtypeStruct((32, points * 2 * HALF, LANES), jnp.bfloat16),
            jax.ShapeDtypeStruct((points,) + fit.shape[1:], fit.dtype),
        ],
        compiler_params=params(),
        cost_estimate=cost(2**18, 2**20),
        name="pack",
    )(band, green_k, fit)


def add(a, b):
    return (a[0] + b[0], a[1] + b[1])


def sub(a, b):
    return (a[0] - b[0], a[1] - b[1])


def turn(a):
    return (-a[1], a[0])


def transform_kernel(x_ref, out_ref, mid_ref):
    for k1 in range(8):
        point = []
        for k2 in range(4):
            rows = x_ref[k1 * 4 + k2].astype(jnp.float32).reshape(4, HALF, LANES)
            a, b = (rows[0], rows[1]), (rows[2], rows[3])
            point.append((add(a, b), sub(a, b)))
        for r3 in range(2):
            y0, y1, y2, y3 = (point[k2][r3] for k2 in range(4))
            s02, d02, s13, d13 = add(y0, y2), sub(y0, y2), add(y1, y3), turn(sub(y1, y3))
            for r2, value in enumerate((add(s02, s13), add(d02, d13), sub(s02, s13), sub(d02, d13))):
                mid_ref[k1, r2, r3, 0] = value[0]
                mid_ref[k1, r2, r3, 1] = value[1]
    root = 0.5**0.5
    scale = 1.0 / 64.0
    for r2 in range(4):
        images = []
        for r3 in range(2):
            re = [mid_ref[k1, r2, r3, 0] for k1 in range(8)]
            im = [mid_ref[k1, r2, r3, 1] for k1 in range(8)]
            p1, p2, p3 = re[1] + re[7], re[2] + re[6], re[3] + re[5]
            q1, q2, q3 = im[1] - im[7], im[2] - im[6], im[3] - im[5]
            even, odd = re[0] + re[4], re[0] - re[4]
            pp, qq = p1 + p3, q1 - q3
            pm, qp = root * (p1 - p3), root * (q1 + q3)
            e_plus, e_minus = even + p2, even - p2
            h0, h1 = odd + pm, odd - pm
            g0, g1 = qp + q2, qp - q2
            images.append(
                (e_plus + pp, h0 - g0, e_minus - qq, h1 - g1, e_plus - pp, h1 + g1, e_minus + qq, h0 + g0)
            )
        for r1 in range(8):
            pair = jnp.concatenate([images[0][r1], images[1][r1]], axis=0) * scale
            out_ref[r1 * 4 + r2] = pair.astype(jnp.bfloat16)


def transform(x):
    return pl.pallas_call(
        transform_kernel,
        in_specs=[VMEM],
        out_specs=VMEM,
        out_shape=jax.ShapeDtypeStruct((32, 2 * HALF, LANES), jnp.bfloat16),
        scratch_shapes=[pltpu.VMEM((8, 4, 2, 2, HALF, LANES), jnp.float32)],
        compiler_params=params(),
        cost_estimate=cost(2**20, 2**20),
        name="transform",
    )(x)


def gram(a, b):
    return lax.dot_general(a, b, (((0,), (0,)), ((), ())), preferred_element_type=jnp.float32)


def partial_kernel(*refs):
    out_ref = refs[-1]
    for s in range(2):
        whole = jnp.concatenate([ref[s] for ref in refs[:-1]], axis=0)
        left, right = whole[:, :LANES], whole[:, LANES:]
        out_ref[s, 0] = gram(left, left)
        out_ref[s, 1] = gram(left, right)
        out_ref[s, 2] = gram(right, right)


def partial_integral(factors):
    return pl.pallas_call(
        partial_kernel,
        in_specs=[VMEM] * len(factors),
        out_specs=VMEM,
        out_shape=jax.ShapeDtypeStruct((2, 3, LANES, LANES), jnp.float32),
        compiler_params=params(),
        cost_estimate=cost(2**27, 2**20),
        name="partial_integral",
    )(*factors)


def sigma_kernel(images_ref, *refs):
    out_ref = refs[-1]
    parts = refs[:-1]
    for s in range(2):
        total = parts[0][s]
        for part in parts[1:]:
            total = total + part[s]
        total = total.astype(jnp.bfloat16)
        green = []
        for jh in range(2):
            tiles = []
            for t in range(TAU):
                for ih in range(2):
                    tile = images_ref[(t * 2 + ih) * 2 + jh].astype(jnp.float32)
                    tiles.append(tile[s * HALF : (s + 1) * HALF])
            green.append(tiles)
        first, second = (jnp.concatenate(tiles, axis=0).astype(jnp.bfloat16) for tiles in green)
        left = (
            jnp.dot(first, total[0], preferred_element_type=jnp.float32)
            + lax.dot_general(second, total[1], (((1,), (1,)), ((), ())), preferred_element_type=jnp.float32),
            jnp.dot(first, total[1], preferred_element_type=jnp.float32)
            + jnp.dot(second, total[2], preferred_element_type=jnp.float32),
        )
        for jh in range(2):
            for t in range(TAU):
                for ih in range(2):
                    at = (t * 2 + ih) * HALF
                    back = green[jh][(TAU - 1 - t) * 2 + ih]
                    out_ref[s, t, ih * HALF : (ih + 1) * HALF, jh * LANES : (jh + 1) * LANES] = (
                        left[jh][at : at + HALF] * back
                    )


def self_energy(images, parts):
    return pl.pallas_call(
        sigma_kernel,
        in_specs=[VMEM] * (1 + len(parts)),
        out_specs=VMEM,
        out_shape=jax.ShapeDtypeStruct((2, TAU, 2 * HALF, 2 * LANES), jnp.float32),
        compiler_params=params(),
        cost_estimate=cost(2**26, 2**20),
        name="self_energy",
    )(images, *parts)


def along_x(value, step):
    pairs = [(o, o // SIDE * SIDE + (o + step) % SIDE) for o in range(SIDE * SIDE)]
    return lax.ppermute(value, "orb", pairs)


def along_y(value, step):
    pairs = [(o, (o + step * SIDE) % (SIDE * SIDE)) for o in range(SIDE * SIDE)]
    return lax.ppermute(value, "orb", pairs)


def per_device(green_k, band_of_image, fit_tensor):
    packed, factor = pack(green_k, band_of_image, fit_tensor)
    factors = [factor] + [along_x(factor, step) for step in (1, 2, 3)]
    block = lax.all_to_all(packed, "img", 0, 0, tiled=True)
    part = partial_integral(factors)
    parts = [part] + [along_y(part, step) for step in (1, 2, 3)]
    images = lax.all_to_all(transform(block), "img", 0, 0, tiled=True)
    return self_energy(images, parts)


def solution(mesh):
    return jax.shard_map(
        per_device,
        mesh=mesh,
        in_specs=(P("img", None, None, "orb", None), P("img"), P(None, "orb", None)),
        out_specs=P("img", None, "orb", None),
        check_vma=False,
    )
```

```python
import jax
import jax.numpy as jnp
from jax import lax
from jax.experimental import pallas as pl
from jax.experimental.pallas import tpu as pltpu
from jax.sharding import PartitionSpec as P

TAU = 8
LANES = 128
HALF = 8
SIDE = 4
VMEM = pl.BlockSpec(memory_space=pltpu.VMEM)
HBM = pl.BlockSpec(memory_space=pltpu.HBM)
CHIPS = (11,10,9,8,7,6,5,4,3,2,1,0,15,14,13,12)
ORDER = [2 * z + core for core in range(2) for z in CHIPS]
PLACE = [ORDER.index(img) for img in range(32)]
LIMIT = 16 * 1024 * 1024


def params(limit=LIMIT):
    return pltpu.CompilerParams(vmem_limit_bytes=limit)


def cost(flops, moved):
    return pl.CostEstimate(flops=flops, bytes_accessed=moved, transcendentals=0)


def pack_kernel(band_hbm, green_hbm, fit_hbm, packed_ref, factor_ref, band, green, sems):
    points = green.shape[0]
    bands = pltpu.make_async_copy(band_hbm, band, sems.at[2 * points])
    bands.start()
    loads = [pltpu.make_async_copy(green_hbm.at[p], green.at[p], sems.at[p]) for p in range(points)]
    for load in loads:
        load.start()
    bands.wait()
    fits = []
    for p in range(points):
        fits.append(pltpu.make_async_copy(fit_hbm.at[band[p]], factor_ref.at[p], sems.at[points + p]))
        fits[p].start()
    for p in range(points):
        loads[p].wait()
        for t in range(TAU):
            for ih in range(2):
                rows = slice(ih * HALF, (ih + 1) * HALF)
                for jh in range(2):
                    cols = slice(jh * LANES, (jh + 1) * LANES)
                    both = green[p, t, :, rows, cols].reshape(2 * HALF, LANES)
                    packed_ref[(t * 2 + ih) * 2 + jh, 2 * HALF * p : 2 * HALF * (p + 1), :] = both.astype(
                        jnp.bfloat16
                    )
    for fit in fits:
        fit.wait()


def pack(green_k, band, fit):
    points = green_k.shape[0]
    return pl.pallas_call(
        pack_kernel,
        in_specs=[HBM] * 3,
        out_specs=[VMEM] * 2,
        out_shape=[
            jax.ShapeDtypeStruct((32, points * 2 * HALF, LANES), jnp.bfloat16),
            jax.ShapeDtypeStruct((points,) + fit.shape[1:], fit.dtype),
        ],
        scratch_shapes=[
            pltpu.SMEM(band.shape, jnp.int32),
            pltpu.VMEM(green_k.shape, jnp.float32),
            pltpu.SemaphoreType.DMA((2 * points + 1,)),
        ],
        compiler_params=params(60 * 1024 * 1024),
        cost_estimate=cost(2**18, 2**20),
        name="pack",
    )(band, green_k, fit)


def add(a, b):
    return (a[0] + b[0], a[1] + b[1])


def sub(a, b):
    return (a[0] - b[0], a[1] - b[1])


def turn(a):
    return (-a[1], a[0])


def transform_kernel(x_ref, out_ref, mid_ref):
    for k1 in range(8):
        point = []
        for k2 in range(4):
            rows = x_ref[PLACE[k1 * 4 + k2]].astype(jnp.float32).reshape(4, HALF, LANES)
            a, b = (rows[0], rows[1]), (rows[2], rows[3])
            point.append((add(a, b), sub(a, b)))
        for r3 in range(2):
            y0, y1, y2, y3 = (point[k2][r3] for k2 in range(4))
            s02, d02, s13, d13 = add(y0, y2), sub(y0, y2), add(y1, y3), turn(sub(y1, y3))
            for r2, value in enumerate((add(s02, s13), add(d02, d13), sub(s02, s13), sub(d02, d13))):
                mid_ref[k1, r2, r3, 0] = value[0]
                mid_ref[k1, r2, r3, 1] = value[1]
    root = 0.5**0.5
    scale = 1.0 / 64.0
    for r2 in range(4):
        images = []
        for r3 in range(2):
            re = [mid_ref[k1, r2, r3, 0] for k1 in range(8)]
            im = [mid_ref[k1, r2, r3, 1] for k1 in range(8)]
            p1, p2, p3 = re[1] + re[7], re[2] + re[6], re[3] + re[5]
            q1, q2, q3 = im[1] - im[7], im[2] - im[6], im[3] - im[5]
            even, odd = re[0] + re[4], re[0] - re[4]
            pp, qq = p1 + p3, q1 - q3
            pm, qp = root * (p1 - p3), root * (q1 + q3)
            e_plus, e_minus = even + p2, even - p2
            h0, h1 = odd + pm, odd - pm
            g0, g1 = qp + q2, qp - q2
            images.append(
                (e_plus + pp, h0 - g0, e_minus - qq, h1 - g1, e_plus - pp, h1 + g1, e_minus + qq, h0 + g0)
            )
        for r1 in range(8):
            pair = jnp.concatenate([images[0][r1], images[1][r1]], axis=0) * scale
            out_ref[PLACE[r1 * 4 + r2]] = pair.astype(jnp.bfloat16)


def transform(x):
    return pl.pallas_call(
        transform_kernel,
        in_specs=[VMEM],
        out_specs=VMEM,
        out_shape=jax.ShapeDtypeStruct((32, 2 * HALF, LANES), jnp.bfloat16),
        scratch_shapes=[pltpu.VMEM((8, 4, 2, 2, HALF, LANES), jnp.float32)],
        compiler_params=params(),
        cost_estimate=cost(2**20, 2**20),
        name="transform",
    )(x)


def gram(a, b):
    return lax.dot_general(a, b, (((0,), (0,)), ((), ())), preferred_element_type=jnp.float32)


def partial_kernel(*refs):
    out_ref = refs[-1]
    for s in range(2):
        whole = jnp.concatenate([ref[s] for ref in refs[:-1]], axis=0)
        left, right = whole[:, :LANES], whole[:, LANES:]
        out_ref[s, 0] = gram(left, left)
        out_ref[s, 1] = gram(left, right)
        out_ref[s, 2] = gram(right, right)


def partial_integral(factors):
    return pl.pallas_call(
        partial_kernel,
        in_specs=[VMEM] * len(factors),
        out_specs=VMEM,
        out_shape=jax.ShapeDtypeStruct((2, 3, LANES, LANES), jnp.float32),
        compiler_params=params(),
        cost_estimate=cost(2**27, 2**20),
        name="partial_integral",
    )(*factors)


def sigma_kernel(images_ref, *refs):
    out_ref = refs[-1]
    parts = refs[:-1]
    for s in range(2):
        total = parts[0][s]
        for part in parts[1:]:
            total = total + part[s]
        total = total.astype(jnp.bfloat16)
        green = []
        for jh in range(2):
            tiles = []
            for t in range(TAU):
                for ih in range(2):
                    tile = images_ref[(t * 2 + ih) * 2 + jh].astype(jnp.float32)
                    tiles.append(tile[s * HALF : (s + 1) * HALF])
            green.append(tiles)
        first, second = (jnp.concatenate(tiles, axis=0).astype(jnp.bfloat16) for tiles in green)
        left = (
            jnp.dot(first, total[0], preferred_element_type=jnp.float32)
            + lax.dot_general(second, total[1], (((1,), (1,)), ((), ())), preferred_element_type=jnp.float32),
            jnp.dot(first, total[1], preferred_element_type=jnp.float32)
            + jnp.dot(second, total[2], preferred_element_type=jnp.float32),
        )
        for jh in range(2):
            for t in range(TAU):
                for ih in range(2):
                    at = (t * 2 + ih) * HALF
                    back = green[jh][(TAU - 1 - t) * 2 + ih]
                    out_ref[s, t, ih * HALF : (ih + 1) * HALF, jh * LANES : (jh + 1) * LANES] = (
                        left[jh][at : at + HALF] * back
                    )


def self_energy(images, parts):
    return pl.pallas_call(
        sigma_kernel,
        in_specs=[VMEM] * (1 + len(parts)),
        out_specs=VMEM,
        out_shape=jax.ShapeDtypeStruct((2, TAU, 2 * HALF, 2 * LANES), jnp.float32),
        compiler_params=params(),
        cost_estimate=cost(2**26, 2**20),
        name="self_energy",
    )(images, *parts)


def lines():
    groups = []
    for img in range(32):
        for at in range(SIDE):
            first, step = (at * SIDE, 1) if img % 2 == 0 else (at, SIDE)
            groups.append([img * SIDE * SIDE + first + step * i for i in range(SIDE)])
    return groups


def exchanged(value, move, turned):
    pairs = []
    for img in range(32):
        for orb in range(SIDE * SIDE):
            y, x = divmod(orb, SIDE)
            if (img + turned) % 2 == 0:
                x = move(x) % SIDE
            else:
                y = move(y) % SIDE
            pairs.append((img * SIDE * SIDE + orb, img * SIDE * SIDE + y * SIDE + x))
    return lax.ppermute(value, ("img", "orb"), pairs)


def per_device(green_k, band_of_image, fit_tensor):
    packed, factor = pack(green_k, band_of_image, fit_tensor)
    block = lax.all_to_all(packed, "img", 0, 0, tiled=True, axis_index_groups=[ORDER])
    part = partial_integral([lax.all_gather(factor, ("img", "orb"), axis=1, tiled=True, axis_index_groups=lines())])
    pair = part + exchanged(part, lambda at: at ^ 1, 1)
    other = exchanged(pair, lambda at: at + 1 if at % 2 else at - 1, 1)
    images = lax.all_to_all(transform(block), "img", 0, 0, tiled=True, axis_index_groups=[ORDER])
    return self_energy(images, [pair, other])


def solution(mesh):
    return jax.shard_map(
        per_device,
        mesh=mesh,
        in_specs=(P("img", None, None, "orb", None), P("img"), P(None, "orb", None)),
        out_specs=P("img", None, "orb", None),
        check_vma=False,
    )
```

```python
import jax
import jax.numpy as jnp
from jax import lax
from jax.experimental import pallas as pl
from jax.experimental.pallas import tpu as pltpu
from jax.sharding import PartitionSpec as P

TAU = 8
LANES = 128
HALF = 8
SIDE = 4
VMEM = pl.BlockSpec(memory_space=pltpu.VMEM)
HBM = pl.BlockSpec(memory_space=pltpu.HBM)
ORDER = [24, 22, 20, 18, 16, 14, 12, 10, 8, 6, 4, 2, 0, 30, 28, 26, 25, 23, 21, 19, 17, 15, 13, 11, 9, 7, 5, 3, 1, 31, 29, 27]
BACK_ORDER = [20, 18, 16, 14, 12, 10, 8, 6, 4, 2, 0, 30, 28, 26, 24, 22, 21, 19, 17, 15, 13, 11, 9, 7, 5, 3, 1, 31, 29, 27, 25, 23]
PLACE = [ORDER.index(img) for img in range(32)]
BACK_PLACE = [BACK_ORDER.index(img) for img in range(32)]
CAME = [BACK_PLACE[img] for img in ORDER]
LIMIT = 16 * 1024 * 1024


def params(limit=LIMIT):
    return pltpu.CompilerParams(vmem_limit_bytes=limit)


def cost(flops, moved):
    return pl.CostEstimate(flops=flops, bytes_accessed=moved, transcendentals=0)


def pack_kernel(band_hbm, green_hbm, fit_hbm, packed_ref, factor_ref, band, green, sems):
    points = green.shape[0]
    bands = pltpu.make_async_copy(band_hbm, band, sems.at[2 * points])
    bands.start()
    loads = [pltpu.make_async_copy(green_hbm.at[p], green.at[p], sems.at[p]) for p in range(points)]
    for load in loads:
        load.start()
    bands.wait()
    fits = []
    for p in range(points):
        fits.append(pltpu.make_async_copy(fit_hbm.at[band[p]], factor_ref.at[p], sems.at[points + p]))
        fits[p].start()
    for p in range(points):
        loads[p].wait()
        for t in range(TAU):
            for ih in range(2):
                rows = slice(ih * HALF, (ih + 1) * HALF)
                for jh in range(2):
                    cols = slice(jh * LANES, (jh + 1) * LANES)
                    both = green[p, t, :, rows, cols].reshape(2 * HALF, LANES)
                    packed_ref[(t * 2 + ih) * 2 + jh, 2 * HALF * p : 2 * HALF * (p + 1), :] = both.astype(
                        jnp.bfloat16
                    )
    for fit in fits:
        fit.wait()


def pack(green_k, band, fit):
    points = green_k.shape[0]
    return pl.pallas_call(
        pack_kernel,
        in_specs=[HBM] * 3,
        out_specs=[VMEM] * 2,
        out_shape=[
            jax.ShapeDtypeStruct((32, points * 2 * HALF, LANES), jnp.bfloat16),
            jax.ShapeDtypeStruct((points,) + fit.shape[1:], fit.dtype),
        ],
        scratch_shapes=[
            pltpu.SMEM(band.shape, jnp.int32),
            pltpu.VMEM(green_k.shape, jnp.float32),
            pltpu.SemaphoreType.DMA((2 * points + 1,)),
        ],
        compiler_params=params(60 * 1024 * 1024),
        cost_estimate=cost(2**18, 2**20),
        name="pack",
    )(band, green_k, fit)


def add(a, b):
    return (a[0] + b[0], a[1] + b[1])


def sub(a, b):
    return (a[0] - b[0], a[1] - b[1])


def turn(a):
    return (-a[1], a[0])


def transform_kernel(x_ref, out_ref, mid_ref):
    for k1 in range(8):
        point = []
        for k2 in range(4):
            rows = x_ref[PLACE[k1 * 4 + k2]].astype(jnp.float32).reshape(4, HALF, LANES)
            a, b = (rows[0], rows[1]), (rows[2], rows[3])
            point.append((add(a, b), sub(a, b)))
        for r3 in range(2):
            y0, y1, y2, y3 = (point[k2][r3] for k2 in range(4))
            s02, d02, s13, d13 = add(y0, y2), sub(y0, y2), add(y1, y3), turn(sub(y1, y3))
            for r2, value in enumerate((add(s02, s13), add(d02, d13), sub(s02, s13), sub(d02, d13))):
                mid_ref[k1, r2, r3, 0] = value[0]
                mid_ref[k1, r2, r3, 1] = value[1]
    root = 0.5**0.5
    scale = 1.0 / 64.0
    for r2 in range(4):
        images = []
        for r3 in range(2):
            re = [mid_ref[k1, r2, r3, 0] for k1 in range(8)]
            im = [mid_ref[k1, r2, r3, 1] for k1 in range(8)]
            p1, p2, p3 = re[1] + re[7], re[2] + re[6], re[3] + re[5]
            q1, q2, q3 = im[1] - im[7], im[2] - im[6], im[3] - im[5]
            even, odd = re[0] + re[4], re[0] - re[4]
            pp, qq = p1 + p3, q1 - q3
            pm, qp = root * (p1 - p3), root * (q1 + q3)
            e_plus, e_minus = even + p2, even - p2
            h0, h1 = odd + pm, odd - pm
            g0, g1 = qp + q2, qp - q2
            images.append(
                (e_plus + pp, h0 - g0, e_minus - qq, h1 - g1, e_plus - pp, h1 + g1, e_minus + qq, h0 + g0)
            )
        for r1 in range(8):
            pair = jnp.concatenate([images[0][r1], images[1][r1]], axis=0) * scale
            out_ref[BACK_PLACE[r1 * 4 + r2]] = pair.astype(jnp.bfloat16)


def transform(x):
    return pl.pallas_call(
        transform_kernel,
        in_specs=[VMEM],
        out_specs=VMEM,
        out_shape=jax.ShapeDtypeStruct((32, 2 * HALF, LANES), jnp.bfloat16),
        scratch_shapes=[pltpu.VMEM((8, 4, 2, 2, HALF, LANES), jnp.float32)],
        compiler_params=params(),
        cost_estimate=cost(2**20, 2**20),
        name="transform",
    )(x)


def gram(a, b):
    return lax.dot_general(a, b, (((0,), (0,)), ((), ())), preferred_element_type=jnp.float32)


def partial_kernel(whole_ref, out_ref):
    row = lax.broadcasted_iota(jnp.int32, (LANES, LANES), 0)
    col = lax.broadcasted_iota(jnp.int32, (LANES, LANES), 1)
    for s in range(2):
        left, right = whole_ref[s, :, :LANES], whole_ref[s, :, LANES:]
        second = gram(right, right)
        out_ref[s, :LANES] = gram(left, right)
        out_ref[s, LANES : 2 * LANES] = jnp.where(row <= col, gram(left, left), second)
        diagonal = jnp.sum(jnp.where(row == col, second, 0.0), axis=0, keepdims=True)
        out_ref[s, 2 * LANES :] = jnp.broadcast_to(diagonal, (HALF, LANES))


def partial_integral(whole):
    return pl.pallas_call(
        partial_kernel,
        in_specs=[VMEM],
        out_specs=VMEM,
        out_shape=jax.ShapeDtypeStruct((2, 2 * LANES + HALF, LANES), jnp.float32),
        compiler_params=params(),
        cost_estimate=cost(2**27, 2**20),
        name="partial_integral",
    )(whole)


def sigma_kernel(images_ref, here_ref, there_ref, out_ref):
    row = lax.broadcasted_iota(jnp.int32, (LANES, LANES), 0)
    col = lax.broadcasted_iota(jnp.int32, (LANES, LANES), 1)
    for s in range(2):
        total = here_ref[s] + there_ref[s]
        mixed = total[:LANES].astype(jnp.bfloat16)
        folded = total[LANES : 2 * LANES]
        flipped = folded.T
        top = jnp.where(row <= col, folded, flipped).astype(jnp.bfloat16)
        low = jnp.where(row < col, flipped, folded)
        low = jnp.where(row == col, jnp.broadcast_to(total[2 * LANES : 2 * LANES + 1], low.shape), low)
        low = low.astype(jnp.bfloat16)
        green = []
        for jh in range(2):
            tiles = []
            for t in range(TAU):
                for ih in range(2):
                    tile = images_ref[CAME[(t * 2 + ih) * 2 + jh]].astype(jnp.float32)
                    tiles.append(tile[s * HALF : (s + 1) * HALF])
            green.append(tiles)
        first, second = (jnp.concatenate(tiles, axis=0).astype(jnp.bfloat16) for tiles in green)
        left = (
            jnp.dot(first, top, preferred_element_type=jnp.float32)
            + lax.dot_general(second, mixed, (((1,), (1,)), ((), ())), preferred_element_type=jnp.float32),
            jnp.dot(first, mixed, preferred_element_type=jnp.float32)
            + jnp.dot(second, low, preferred_element_type=jnp.float32),
        )
        for jh in range(2):
            for t in range(TAU):
                for ih in range(2):
                    at = (t * 2 + ih) * HALF
                    back = green[jh][(TAU - 1 - t) * 2 + ih]
                    out_ref[s, t, ih * HALF : (ih + 1) * HALF, jh * LANES : (jh + 1) * LANES] = (
                        left[jh][at : at + HALF] * back
                    )


def self_energy(images, here, there):
    return pl.pallas_call(
        sigma_kernel,
        in_specs=[VMEM] * 3,
        out_specs=VMEM,
        out_shape=jax.ShapeDtypeStruct((2, TAU, 2 * HALF, 2 * LANES), jnp.float32),
        compiler_params=params(),
        cost_estimate=cost(2**26, 2**20),
        name="self_energy",
    )(images, here, there)


def lines():
    groups = []
    for img in range(32):
        for at in range(SIDE):
            first, step = (at * SIDE, 1) if img % 2 == 0 else (at, SIDE)
            groups.append([img * SIDE * SIDE + first + step * i for i in range(SIDE)])
    return groups


def exchanged(value, move, turned):
    pairs = []
    for img in range(32):
        for orb in range(SIDE * SIDE):
            y, x = divmod(orb, SIDE)
            if (img + turned) % 2 == 0:
                x = move(x) % SIDE
            else:
                y = move(y) % SIDE
            pairs.append((img * SIDE * SIDE + orb, img * SIDE * SIDE + y * SIDE + x))
    return lax.ppermute(value, ("img", "orb"), pairs)


def per_device(green_k, band_of_image, fit_tensor):
    packed, factor = pack(green_k, band_of_image, fit_tensor)
    block = lax.all_to_all(packed, "img", 0, 0, tiled=True, axis_index_groups=[ORDER])
    part = partial_integral(lax.all_gather(factor, ("img", "orb"), axis=1, tiled=True, axis_index_groups=lines()))
    pair = part + exchanged(part, lambda at: at ^ 1, 1)
    other = exchanged(pair, lambda at: at + 1 if at % 2 else at - 1, 1)
    images = lax.all_to_all(transform(block), "img", 0, 0, tiled=True, axis_index_groups=[BACK_ORDER])
    return self_energy(images, pair, other)


def solution(mesh):
    return jax.shard_map(
        per_device,
        mesh=mesh,
        in_specs=(P("img", None, None, "orb", None), P("img"), P(None, "orb", None)),
        out_specs=P("img", None, "orb", None),
        check_vma=False,
    )
```

```python
import jax
import jax.numpy as jnp
from jax import lax
from jax.experimental import pallas as pl
from jax.experimental.pallas import tpu as pltpu
from jax.sharding import PartitionSpec as P

TAU = 8
LANES = 128
HALF = 8
SIDE = 4
VMEM = pl.BlockSpec(memory_space=pltpu.VMEM)
HBM = pl.BlockSpec(memory_space=pltpu.HBM)
ORDER = [24, 22, 20, 18, 16, 14, 12, 10, 8, 6, 4, 2, 0, 30, 28, 26, 25, 23, 21, 19, 17, 15, 13, 11, 9, 7, 5, 3, 1, 31, 29, 27]
BACK_ORDER = [20, 18, 16, 14, 12, 10, 8, 6, 4, 2, 0, 30, 28, 26, 24, 22, 21, 19, 17, 15, 13, 11, 9, 7, 5, 3, 1, 31, 29, 27, 25, 23]
PLACE = [ORDER.index(img) for img in range(32)]
BACK_PLACE = [BACK_ORDER.index(img) for img in range(32)]
CAME = [BACK_PLACE[img] for img in ORDER]
LIMIT = 16 * 1024 * 1024


def params(limit=LIMIT):
    return pltpu.CompilerParams(vmem_limit_bytes=limit)


def cost(flops, moved):
    return pl.CostEstimate(flops=flops, bytes_accessed=moved, transcendentals=0)


def pack_kernel(band_hbm, green_hbm, fit_hbm, packed_ref, factor_ref, band, green, sems):
    points = green.shape[0]
    bands = pltpu.make_async_copy(band_hbm, band, sems.at[2 * points])
    bands.start()
    load = pltpu.make_async_copy(green_hbm, green, sems.at[0])
    load.start()
    bands.wait()
    fits = []
    for p in range(points):
        fits.append(pltpu.make_async_copy(fit_hbm.at[band[p]], factor_ref.at[p], sems.at[points + p]))
        fits[p].start()
    load.wait()
    for p in range(points):
        for t in range(TAU):
            for ih in range(2):
                rows = slice(ih * HALF, (ih + 1) * HALF)
                for jh in range(2):
                    cols = slice(jh * LANES, (jh + 1) * LANES)
                    both = green[p, t, :, rows, cols].reshape(2 * HALF, LANES)
                    packed_ref[(t * 2 + ih) * 2 + jh, 2 * HALF * p : 2 * HALF * (p + 1), :] = both.astype(
                        jnp.bfloat16
                    )
    for fit in fits:
        fit.wait()


def pack(green_k, band, fit):
    points = green_k.shape[0]
    return pl.pallas_call(
        pack_kernel,
        in_specs=[HBM] * 3,
        out_specs=[VMEM] * 2,
        out_shape=[
            jax.ShapeDtypeStruct((32, points * 2 * HALF, LANES), jnp.bfloat16),
            jax.ShapeDtypeStruct((points,) + fit.shape[1:], fit.dtype),
        ],
        scratch_shapes=[
            pltpu.SMEM(band.shape, jnp.int32),
            pltpu.VMEM(green_k.shape, jnp.float32),
            pltpu.SemaphoreType.DMA((2 * points + 1,)),
        ],
        compiler_params=params(60 * 1024 * 1024),
        cost_estimate=cost(2**18, 2**20),
        name="pack",
    )(band, green_k, fit)


def add(a, b):
    return (a[0] + b[0], a[1] + b[1])


def sub(a, b):
    return (a[0] - b[0], a[1] - b[1])


def turn(a):
    return (-a[1], a[0])


def transform_kernel(x_ref, out_ref, mid_ref):
    for k1 in range(8):
        point = []
        for k2 in range(4):
            rows = x_ref[PLACE[k1 * 4 + k2]].astype(jnp.float32).reshape(4, HALF, LANES)
            a, b = (rows[0], rows[1]), (rows[2], rows[3])
            point.append((add(a, b), sub(a, b)))
        for r3 in range(2):
            y0, y1, y2, y3 = (point[k2][r3] for k2 in range(4))
            s02, d02, s13, d13 = add(y0, y2), sub(y0, y2), add(y1, y3), turn(sub(y1, y3))
            for r2, value in enumerate((add(s02, s13), add(d02, d13), sub(s02, s13), sub(d02, d13))):
                mid_ref[k1, r2, r3, 0] = value[0]
                mid_ref[k1, r2, r3, 1] = value[1]
    root = 0.5**0.5
    scale = 1.0 / 64.0
    for r2 in range(4):
        images = []
        for r3 in range(2):
            re = [mid_ref[k1, r2, r3, 0] for k1 in range(8)]
            im = [mid_ref[k1, r2, r3, 1] for k1 in range(8)]
            p1, p2, p3 = re[1] + re[7], re[2] + re[6], re[3] + re[5]
            q1, q2, q3 = im[1] - im[7], im[2] - im[6], im[3] - im[5]
            even, odd = re[0] + re[4], re[0] - re[4]
            pp, qq = p1 + p3, q1 - q3
            pm, qp = root * (p1 - p3), root * (q1 + q3)
            e_plus, e_minus = even + p2, even - p2
            h0, h1 = odd + pm, odd - pm
            g0, g1 = qp + q2, qp - q2
            images.append(
                (e_plus + pp, h0 - g0, e_minus - qq, h1 - g1, e_plus - pp, h1 + g1, e_minus + qq, h0 + g0)
            )
        for r1 in range(8):
            pair = jnp.concatenate([images[0][r1], images[1][r1]], axis=0) * scale
            out_ref[BACK_PLACE[r1 * 4 + r2]] = pair.astype(jnp.bfloat16)


def transform(x):
    return pl.pallas_call(
        transform_kernel,
        in_specs=[VMEM],
        out_specs=VMEM,
        out_shape=jax.ShapeDtypeStruct((32, 2 * HALF, LANES), jnp.bfloat16),
        scratch_shapes=[pltpu.VMEM((8, 4, 2, 2, HALF, LANES), jnp.float32)],
        compiler_params=params(),
        cost_estimate=cost(2**20, 2**20),
        name="transform",
    )(x)


def gram(a, b):
    return lax.dot_general(a, b, (((0,), (0,)), ((), ())), preferred_element_type=jnp.float32)


def partial_kernel(whole_ref, out_ref):
    row = lax.broadcasted_iota(jnp.int32, (LANES, LANES), 0)
    col = lax.broadcasted_iota(jnp.int32, (LANES, LANES), 1)
    for s in range(2):
        left, right = whole_ref[s, :, :LANES], whole_ref[s, :, LANES:]
        second = gram(right, right)
        out_ref[s, :LANES] = gram(left, right)
        out_ref[s, LANES : 2 * LANES] = jnp.where(row <= col, gram(left, left), second)
        diagonal = jnp.sum(jnp.where(row == col, second, 0.0), axis=0, keepdims=True)
        out_ref[s, 2 * LANES :] = jnp.broadcast_to(diagonal, (HALF, LANES))


def partial_integral(whole):
    return pl.pallas_call(
        partial_kernel,
        in_specs=[VMEM],
        out_specs=VMEM,
        out_shape=jax.ShapeDtypeStruct((2, 2 * LANES + HALF, LANES), jnp.float32),
        compiler_params=params(),
        cost_estimate=cost(2**27, 2**20),
        name="partial_integral",
    )(whole)


def sigma_kernel(images_ref, here_ref, there_ref, out_ref):
    row = lax.broadcasted_iota(jnp.int32, (LANES, LANES), 0)
    col = lax.broadcasted_iota(jnp.int32, (LANES, LANES), 1)
    for s in range(2):
        total = here_ref[s] + there_ref[s]
        mixed = total[:LANES].astype(jnp.bfloat16)
        turned = total[:LANES].T.astype(jnp.bfloat16)
        folded = total[LANES : 2 * LANES]
        flipped = folded.T
        top = jnp.where(row <= col, folded, flipped).astype(jnp.bfloat16)
        low = jnp.where(row < col, flipped, folded)
        low = jnp.where(row == col, jnp.broadcast_to(total[2 * LANES : 2 * LANES + 1], low.shape), low)
        low = low.astype(jnp.bfloat16)
        green = []
        for jh in range(2):
            tiles = []
            for t in range(TAU):
                for ih in range(2):
                    tile = images_ref[CAME[(t * 2 + ih) * 2 + jh]].astype(jnp.float32)
                    tiles.append(tile[s * HALF : (s + 1) * HALF])
            green.append(tiles)
        first, second = (jnp.concatenate(tiles, axis=0).astype(jnp.bfloat16) for tiles in green)
        whole = jnp.concatenate(
            [jnp.concatenate([top, mixed], axis=1), jnp.concatenate([turned, low], axis=1)], axis=0
        )
        product = jnp.dot(jnp.concatenate([first, second], axis=1), whole, preferred_element_type=jnp.float32)
        left = (product[:, :LANES], product[:, LANES:])
        for jh in range(2):
            for t in range(TAU):
                for ih in range(2):
                    at = (t * 2 + ih) * HALF
                    back = green[jh][(TAU - 1 - t) * 2 + ih]
                    out_ref[s, t, ih * HALF : (ih + 1) * HALF, jh * LANES : (jh + 1) * LANES] = (
                        left[jh][at : at + HALF] * back
                    )


def self_energy(images, here, there):
    return pl.pallas_call(
        sigma_kernel,
        in_specs=[VMEM] * 3,
        out_specs=VMEM,
        out_shape=jax.ShapeDtypeStruct((2, TAU, 2 * HALF, 2 * LANES), jnp.float32),
        compiler_params=params(),
        cost_estimate=cost(2**26, 2**20),
        name="self_energy",
    )(images, here, there)


def lines():
    groups = []
    for img in range(32):
        for at in range(SIDE):
            first, step = (at * SIDE, 1) if img % 2 == 0 else (at, SIDE)
            groups.append([img * SIDE * SIDE + first + step * i for i in range(SIDE)])
    return groups


def exchanged(value, move, turned):
    pairs = []
    for img in range(32):
        for orb in range(SIDE * SIDE):
            y, x = divmod(orb, SIDE)
            if (img + turned) % 2 == 0:
                x = move(x) % SIDE
            else:
                y = move(y) % SIDE
            pairs.append((img * SIDE * SIDE + orb, img * SIDE * SIDE + y * SIDE + x))
    return lax.ppermute(value, ("img", "orb"), pairs)


def per_device(green_k, band_of_image, fit_tensor):
    packed, factor = pack(green_k, band_of_image, fit_tensor)
    block = lax.all_to_all(packed, "img", 0, 0, tiled=True, axis_index_groups=[ORDER])
    part = partial_integral(lax.all_gather(factor, ("img", "orb"), axis=1, tiled=True, axis_index_groups=lines()))
    pair = part + exchanged(part, lambda at: at ^ 1, 1)
    other = exchanged(pair, lambda at: at + 1 if at % 2 else at - 1, 1)
    images = lax.all_to_all(transform(block), "img", 0, 0, tiled=True, axis_index_groups=[BACK_ORDER])
    return self_energy(images, pair, other)


def solution(mesh):
    return jax.shard_map(
        per_device,
        mesh=mesh,
        in_specs=(P("img", None, None, "orb", None), P("img"), P(None, "orb", None)),
        out_specs=P("img", None, "orb", None),
        check_vma=False,
    )
```

```python
import jax
import jax.numpy as jnp
from jax import lax
from jax.experimental import pallas as pl
from jax.experimental.pallas import tpu as pltpu
from jax.sharding import PartitionSpec as P

TAU = 8
LANES = 128
HALF = 8
SIDE = 4
VMEM = pl.BlockSpec(memory_space=pltpu.VMEM)
HBM = pl.BlockSpec(memory_space=pltpu.HBM)
ORDER = [24, 22, 20, 18, 16, 14, 12, 10, 8, 6, 4, 2, 0, 30, 28, 26, 25, 23, 21, 19, 17, 15, 13, 11, 9, 7, 5, 3, 1, 31, 29, 27]
BACK_ORDER = [18, 19, 16, 17, 14, 15, 12, 13, 10, 11, 8, 9, 6, 7, 4, 5, 2, 3, 0, 1, 30, 31, 28, 29, 26, 27, 24, 25, 22, 23, 20, 21]
PLACE = [ORDER.index(img) for img in range(32)]
BACK_PLACE = [BACK_ORDER.index(img) for img in range(32)]
CAME = [BACK_PLACE[img] for img in ORDER]
LIMIT = 16 * 1024 * 1024


def params(limit=LIMIT):
    return pltpu.CompilerParams(vmem_limit_bytes=limit)


def cost(flops, moved):
    return pl.CostEstimate(flops=flops, bytes_accessed=moved, transcendentals=0)


def pack_kernel(band_hbm, green_hbm, fit_hbm, packed_ref, factor_ref, band, green, sems):
    points = green.shape[0]
    bands = pltpu.make_async_copy(band_hbm, band, sems.at[2 * points])
    bands.start()
    load = pltpu.make_async_copy(green_hbm, green, sems.at[0])
    load.start()
    bands.wait()
    fits = []
    for p in range(points):
        fits.append(pltpu.make_async_copy(fit_hbm.at[band[p]], factor_ref.at[p], sems.at[points + p]))
        fits[p].start()
    load.wait()
    for p in range(points):
        for t in range(TAU):
            for ih in range(2):
                rows = slice(ih * HALF, (ih + 1) * HALF)
                for jh in range(2):
                    cols = slice(jh * LANES, (jh + 1) * LANES)
                    both = green[p, t, :, rows, cols].reshape(2 * HALF, LANES)
                    packed_ref[(t * 2 + ih) * 2 + jh, 2 * HALF * p : 2 * HALF * (p + 1), :] = both.astype(
                        jnp.bfloat16
                    )
    for fit in fits:
        fit.wait()


def pack(green_k, band, fit):
    points = green_k.shape[0]
    return pl.pallas_call(
        pack_kernel,
        in_specs=[HBM] * 3,
        out_specs=[VMEM] * 2,
        out_shape=[
            jax.ShapeDtypeStruct((32, points * 2 * HALF, LANES), jnp.bfloat16),
            jax.ShapeDtypeStruct((points,) + fit.shape[1:], fit.dtype),
        ],
        scratch_shapes=[
            pltpu.SMEM(band.shape, jnp.int32),
            pltpu.VMEM(green_k.shape, jnp.float32),
            pltpu.SemaphoreType.DMA((2 * points + 1,)),
        ],
        compiler_params=params(60 * 1024 * 1024),
        cost_estimate=cost(2**18, 2**20),
        name="pack",
    )(band, green_k, fit)


def add(a, b):
    return (a[0] + b[0], a[1] + b[1])


def sub(a, b):
    return (a[0] - b[0], a[1] - b[1])


def turn(a):
    return (-a[1], a[0])


def transform_kernel(x_ref, out_ref, mid_ref):
    for k1 in range(8):
        point = []
        for k2 in range(4):
            rows = x_ref[PLACE[k1 * 4 + k2]].astype(jnp.float32).reshape(4, HALF, LANES)
            a, b = (rows[0], rows[1]), (rows[2], rows[3])
            point.append((add(a, b), sub(a, b)))
        for r3 in range(2):
            y0, y1, y2, y3 = (point[k2][r3] for k2 in range(4))
            s02, d02, s13, d13 = add(y0, y2), sub(y0, y2), add(y1, y3), turn(sub(y1, y3))
            for r2, value in enumerate((add(s02, s13), add(d02, d13), sub(s02, s13), sub(d02, d13))):
                mid_ref[k1, r2, r3, 0] = value[0]
                mid_ref[k1, r2, r3, 1] = value[1]
    root = 0.5**0.5
    scale = 1.0 / 64.0
    for r2 in range(4):
        images = []
        for r3 in range(2):
            re = [mid_ref[k1, r2, r3, 0] for k1 in range(8)]
            im = [mid_ref[k1, r2, r3, 1] for k1 in range(8)]
            p1, p2, p3 = re[1] + re[7], re[2] + re[6], re[3] + re[5]
            q1, q2, q3 = im[1] - im[7], im[2] - im[6], im[3] - im[5]
            even, odd = re[0] + re[4], re[0] - re[4]
            pp, qq = p1 + p3, q1 - q3
            pm, qp = root * (p1 - p3), root * (q1 + q3)
            e_plus, e_minus = even + p2, even - p2
            h0, h1 = odd + pm, odd - pm
            g0, g1 = qp + q2, qp - q2
            images.append(
                (e_plus + pp, h0 - g0, e_minus - qq, h1 - g1, e_plus - pp, h1 + g1, e_minus + qq, h0 + g0)
            )
        for r1 in range(8):
            pair = jnp.concatenate([images[0][r1], images[1][r1]], axis=0) * scale
            out_ref[BACK_PLACE[r1 * 4 + r2]] = pair.astype(jnp.bfloat16)


def transform(x):
    return pl.pallas_call(
        transform_kernel,
        in_specs=[VMEM],
        out_specs=VMEM,
        out_shape=jax.ShapeDtypeStruct((32, 2 * HALF, LANES), jnp.bfloat16),
        scratch_shapes=[pltpu.VMEM((8, 4, 2, 2, HALF, LANES), jnp.float32)],
        compiler_params=params(),
        cost_estimate=cost(2**20, 2**20),
        name="transform",
    )(x)


def gram(a, b):
    return lax.dot_general(a, b, (((0,), (0,)), ((), ())), preferred_element_type=jnp.float32)


def partial_kernel(whole_ref, out_ref):
    row = lax.broadcasted_iota(jnp.int32, (LANES, LANES), 0)
    col = lax.broadcasted_iota(jnp.int32, (LANES, LANES), 1)
    for s in range(2):
        left, right = whole_ref[s, :, :LANES], whole_ref[s, :, LANES:]
        second = gram(right, right)
        out_ref[s, :LANES] = gram(left, right)
        out_ref[s, LANES : 2 * LANES] = jnp.where(row <= col, gram(left, left), second)
        diagonal = jnp.sum(jnp.where(row == col, second, 0.0), axis=0, keepdims=True)
        out_ref[s, 2 * LANES :] = jnp.broadcast_to(diagonal, (HALF, LANES))


def partial_integral(whole):
    return pl.pallas_call(
        partial_kernel,
        in_specs=[VMEM],
        out_specs=VMEM,
        out_shape=jax.ShapeDtypeStruct((2, 2 * LANES + HALF, LANES), jnp.float32),
        compiler_params=params(),
        cost_estimate=cost(2**27, 2**20),
        name="partial_integral",
    )(whole)


def sigma_kernel(images_ref, here_ref, there_ref, out_ref):
    row = lax.broadcasted_iota(jnp.int32, (LANES, LANES), 0)
    col = lax.broadcasted_iota(jnp.int32, (LANES, LANES), 1)
    for s in range(2):
        total = here_ref[s] + there_ref[s]
        mixed = total[:LANES].astype(jnp.bfloat16)
        turned = total[:LANES].T.astype(jnp.bfloat16)
        folded = total[LANES : 2 * LANES]
        flipped = folded.T
        top = jnp.where(row <= col, folded, flipped).astype(jnp.bfloat16)
        low = jnp.where(row < col, flipped, folded)
        low = jnp.where(row == col, jnp.broadcast_to(total[2 * LANES : 2 * LANES + 1], low.shape), low)
        low = low.astype(jnp.bfloat16)
        green = []
        for jh in range(2):
            tiles = []
            for t in range(TAU):
                for ih in range(2):
                    tile = images_ref[CAME[(t * 2 + ih) * 2 + jh]].astype(jnp.float32)
                    tiles.append(tile[s * HALF : (s + 1) * HALF])
            green.append(tiles)
        first, second = (jnp.concatenate(tiles, axis=0).astype(jnp.bfloat16) for tiles in green)
        whole = jnp.concatenate(
            [jnp.concatenate([top, mixed], axis=1), jnp.concatenate([turned, low], axis=1)], axis=0
        )
        product = jnp.dot(jnp.concatenate([first, second], axis=1), whole, preferred_element_type=jnp.float32)
        left = (product[:, :LANES], product[:, LANES:])
        for jh in range(2):
            for t in range(TAU):
                for ih in range(2):
                    at = (t * 2 + ih) * HALF
                    back = green[jh][(TAU - 1 - t) * 2 + ih]
                    out_ref[s, t, ih * HALF : (ih + 1) * HALF, jh * LANES : (jh + 1) * LANES] = (
                        left[jh][at : at + HALF] * back
                    )


def self_energy(images, here, there):
    return pl.pallas_call(
        sigma_kernel,
        in_specs=[VMEM] * 3,
        out_specs=VMEM,
        out_shape=jax.ShapeDtypeStruct((2, TAU, 2 * HALF, 2 * LANES), jnp.float32),
        compiler_params=params(),
        cost_estimate=cost(2**26, 2**20),
        name="self_energy",
    )(images, here, there)


def lines():
    groups = []
    for img in range(32):
        for at in range(SIDE):
            first, step = (at * SIDE, 1) if img % 2 == 0 else (at, SIDE)
            groups.append([img * SIDE * SIDE + first + step * i for i in range(SIDE)])
    return groups


def exchanged(value, move, turned):
    pairs = []
    for img in range(32):
        for orb in range(SIDE * SIDE):
            y, x = divmod(orb, SIDE)
            if (img + turned) % 2 == 0:
                x = move(x) % SIDE
            else:
                y = move(y) % SIDE
            pairs.append((img * SIDE * SIDE + orb, img * SIDE * SIDE + y * SIDE + x))
    return lax.ppermute(value, ("img", "orb"), pairs)


def per_device(green_k, band_of_image, fit_tensor):
    packed, factor = pack(green_k, band_of_image, fit_tensor)
    block = lax.all_to_all(packed, "img", 0, 0, tiled=True, axis_index_groups=[ORDER])
    part = partial_integral(lax.all_gather(factor, ("img", "orb"), axis=1, tiled=True, axis_index_groups=lines()))
    pair = part + exchanged(part, lambda at: at ^ 1, 1)
    other = exchanged(pair, lambda at: at + 1 if at % 2 else at - 1, 1)
    images = lax.all_to_all(transform(block), "img", 0, 0, tiled=True, axis_index_groups=[BACK_ORDER])
    return self_energy(images, pair, other)


def solution(mesh):
    return jax.shard_map(
        per_device,
        mesh=mesh,
        in_specs=(P("img", None, None, "orb", None), P("img"), P(None, "orb", None)),
        out_specs=P("img", None, "orb", None),
        check_vma=False,
    )
```
